768 devices in a mesh: pair: 192 (over y, z, core), virt: 4 (over x).
Axes of the slice: x: 4, y: 8, z: 12, core: 2. Of those that a mesh axis runs over, the one named last changes fastest.
Arguments:
- amplitudes: bfloat16 [192, 4, 48, 128, 128], P('pair', 'virt'), may hold values from -6 to 6
- offsets: int32 [192, 4, 48, 1], P('pair', 'virt'), may hold values from 0 to 4; in each aligned block of 48 rows (0 to 47, 48 to 95, ..., all dimensions but the last counted through in order) at most 16 rows name the same one
- row_blocks: int32 [192, 4, 48], P('pair', 'virt'), may hold values from 0 to 3
- k_blocks: int32 [192, 4, 48], P('pair', 'virt'), may hold values from 0 to 7
- screen: int32 [192, 4, 48], P('pair', 'virt'), may hold values 0 or 1
- integrals: bfloat16 [192, 4096, 1024], P('pair', 'virt'), may hold values from -0.125 to 0.125
- row_gaps: float32 [98304], P('pair'), may hold values from 0.5 to 4
- col_gaps: float32 [1024], P('virt'), may hold values from 0.5 to 4
Outputs:
- update: float32 [98304, 1024], P('pair', 'virt')
The draws below stay inside these ranges and needn't reach their ends.
Inputs may be any that keep to these rules, and one draw needn't show every extreme that they name: `offsets`: among the tiles of one device no offset value occurs more than 16 times, and some value reaches 16.
All inputs are finite; a program needn't handle non-finite values. No bound on the sum of `screen` on one device may be relied on, other than what follows from the above.
Results may differ from the reference program's by a relative error of at most 0.0025.
Values may be sent and summed in bfloat16 or wider, within the bound.
A program may use at most 32 MiB of HBM per device.

```python
import math
import jax
import jax.numpy as jnp
import numpy as np
from jax import lax

TILE = 128
SLOTS = 48
REACH = 2
CAPD = 16
KB_DEV = 8
ROWB = 4
JCOL = 1024
N_PAIR = 192
N_VIRT = 4


def touch_ends(array, key, low, high):
    dims = array.shape
    place = [jax.random.randint(jax.random.fold_in(key, axis), (), 0, dims[axis]) for axis in range(len(dims))]
    array = array.at[tuple(place)].set(low)
    longest = dims.index(max(dims))
    place[longest] = (place[longest] + 1) % dims[longest]
    return array.at[tuple(place)].set(high)


def shard_levels(key, dims, cuts, least, high):
    factor_of = 1.0
    for position, blocks in cuts:
        steps = jax.random.uniform(jax.random.fold_in(jax.random.fold_in(key, 6), position), (blocks,), jnp.float32, least / len(cuts), high / len(cuts))
        factor_of = factor_of * jnp.repeat(jnp.exp(steps), dims[position] // blocks).reshape((-1,) + (1,) * (len(dims) - 1 - position))
    return factor_of


def shared_out(own_key, own, number, rows, amount, top, limit, slope):
    ranking = jax.random.permutation(own_key, amount)
    packed, usual = load_shares(amount, rows * top, limit, slope, True), load_shares(amount, rows * top, limit, slope, False)
    places = jnp.arange(amount)

    def named(sizes, rotation):
        used = int((sizes > 0).sum())
        fixed = max(1, used // 4)
        shifted = fixed + (places - fixed + rotation * (used - fixed)) % max(1, amount - fixed)
        return jnp.zeros((amount,), jnp.int32).at[ranking[jnp.where(places < fixed, places, shifted)]].set(jnp.asarray(sizes, jnp.int32))

    sizes = jnp.where(number % 4 == 0, named(packed, number // 4), named(usual, number - number // 4 - 1))
    mixed = jax.random.permutation(jax.random.fold_in(own, 3), amount)
    giver, sink = mixed[0:amount // 2 * 2:2], mixed[1:amount // 2 * 2:2]
    room = jnp.minimum(sizes[giver] - 1, limit - sizes[sink]) // 2
    room = jnp.where((giver == ranking[0]) | (sink == ranking[0]) | (sizes[sink] == 0), 0, jnp.maximum(room, 0))
    shifted = jax.random.randint(jax.random.fold_in(own, 4), (amount // 2,), 0, 1 << 20) % (room + 1)
    sizes = sizes.at[giver].add(-shifted).at[sink].add(shifted)
    members = jnp.searchsorted(jnp.cumsum(sizes), jnp.arange(rows * top), side="right").astype(jnp.int32)
    table = members.reshape(top, rows).T
    table = table[jax.random.permutation(jax.random.fold_in(own, 1), rows)]
    rotation = jax.random.randint(jax.random.fold_in(own, 2), (rows, 1), 0, top)
    return jnp.take_along_axis(table, (jnp.arange(top)[None, :] + rotation) % top, axis=1)


def load_shares(count, total, most, slope, full):
    portions = [(1 << 20) // math.isqrt(rank ** slope) + 1 for rank in range(1, count + 1)]
    largest = most if full else min(most, max(-(-total // count), total * portions[0] // sum(portions)))
    least = 1 if total - largest >= count - 1 else 0
    counts, rest = [largest] + [least] * (count - 1), total - largest - least * (count - 1)
    while rest > 0:
        candidates = [i for i in range(1, count) if counts[i] < largest] or [i for i in range(1, count) if counts[i] < most]
        mass, left = sum([portions[i] for i in candidates]), rest
        for i in candidates:
            addition = min(most - counts[i], max(1, left * portions[i] // mass), rest)
            counts[i] = counts[i] + addition
            rest = rest - addition
    return np.array(counts)


def normal_values(stream_key, shape, width, limit, cuts=(), kind=jnp.bfloat16):
    array = jax.random.normal(stream_key, shape, jnp.float32) * width
    if len(cuts) > 0:
        array = shard_levels(stream_key, shape, cuts, -0.22, 0.18) * array
    return jnp.clip(array, min=-limit, max=limit).astype(kind)


def setup_inputs(seed: int = 0) -> dict:
    arg_keys = jax.random.split(jax.random.key(seed), 9)
    amplitudes = normal_values(arg_keys[0], (N_PAIR, N_VIRT, SLOTS, TILE, TILE), 1.0, 6.0, ((0, 192), (1, 4)))
    offsets_keys = jax.random.split(jax.random.fold_in(arg_keys[1], 1), N_PAIR * N_VIRT * SLOTS // SLOTS)
    offsets_turns = jax.random.permutation(jax.random.fold_in(arg_keys[1], 3), N_PAIR * N_VIRT * SLOTS // SLOTS)
    offsets = jax.vmap(lambda own, number: shared_out(jax.random.fold_in(arg_keys[1], 2), own, number, SLOTS, 2 * REACH + 1, 1, CAPD, 2))(offsets_keys, offsets_turns).reshape((N_PAIR, N_VIRT, SLOTS, 1))
    row_blocks = touch_ends(jax.random.randint(arg_keys[2], (N_PAIR, N_VIRT, SLOTS), 0, ROWB), jax.random.fold_in(arg_keys[2], 1), 0, ROWB - 1).astype(jnp.int32)
    k_blocks = touch_ends(jax.random.randint(arg_keys[3], (N_PAIR, N_VIRT, SLOTS), 0, KB_DEV), jax.random.fold_in(arg_keys[3], 1), 0, KB_DEV - 1).astype(jnp.int32)
    screen = touch_ends((jax.random.randint(arg_keys[4], (N_PAIR, N_VIRT, SLOTS), 0, 4) < 3).astype(jnp.int32), jax.random.fold_in(arg_keys[4], 1), 0, 1)
    integrals = normal_values(arg_keys[5], (N_PAIR, N_VIRT * KB_DEV * TILE, JCOL), (TILE * KB_DEV * N_VIRT // 2) ** -0.5, 0.125, ((0, 192), (1, 4)))
    row_gaps = jnp.clip(jnp.exp(math.log(4.0) - 2.0794415 * jax.random.uniform(arg_keys[6], (N_PAIR * ROWB * TILE,), jnp.float32) ** shard_levels(arg_keys[6], (N_PAIR * ROWB * TILE,), ((0, 192),), -0.2, 0.2)), 0.5, 4.0)
    col_gaps = jnp.clip(jnp.exp(math.log(4.0) - 2.0794415 * jax.random.uniform(arg_keys[7], (JCOL,), jnp.float32) ** shard_levels(arg_keys[7], (JCOL,), ((0, 4),), -0.2, 0.2)), 0.5, 4.0)
    return {"amplitudes": amplitudes, "offsets": offsets, "row_blocks": row_blocks, "k_blocks": k_blocks, "screen": screen, "integrals": integrals, "row_gaps": row_gaps, "col_gaps": col_gaps}


def reference(amplitudes, offsets, row_blocks, k_blocks, screen, integrals, row_gaps, col_gaps):
    window_len = 2 * REACH + 1
    tile_offsets = offsets[..., 0]

    def owner_rows(owner):
        sources = (owner + jnp.arange(window_len, dtype=jnp.int32) - REACH) % N_PAIR
        tiles = jnp.take(amplitudes, sources, axis=0).astype(jnp.float32)
        near_off = jnp.take(tile_offsets, sources, axis=0)
        near_rows = jnp.take(row_blocks, sources, axis=0)
        near_ks = jnp.take(k_blocks, sources, axis=0)
        near_screen = jnp.take(screen, sources, axis=0)
        expected = (2 * REACH - jnp.arange(window_len, dtype=jnp.int32))[:, None, None]
        wanted = (near_off == expected) & (near_screen == 1)
        block_index = near_rows * KB_DEV + near_ks
        targets = jnp.arange(ROWB * KB_DEV, dtype=jnp.int32)[:, None, None, None]
        selector = ((block_index[None] == targets) & wanted[None]).astype(jnp.float32)
        blocks = jnp.einsum('bwvs,wvsxy->vbxy', selector, tiles, precision=lax.Precision.HIGHEST).astype(jnp.bfloat16)
        blocks = blocks.reshape(N_VIRT, ROWB, KB_DEV, TILE, TILE).transpose(0, 1, 3, 2, 4)
        blocks = blocks.reshape(N_VIRT, ROWB * TILE, KB_DEV * TILE)
        resident = lax.dynamic_index_in_dim(integrals, owner, 0, keepdims=False)
        resident = resident.reshape(N_VIRT, KB_DEV * TILE, JCOL)
        cycle_term = jnp.einsum('vmk,vkn->mn', blocks.astype(jnp.float32), resident.astype(jnp.float32), precision=lax.Precision.HIGHEST)
        owner_gaps = lax.dynamic_slice_in_dim(row_gaps, owner * ROWB * TILE, ROWB * TILE)
        return cycle_term / (owner_gaps[:, None] + col_gaps[None, :])

    result = lax.map(owner_rows, jnp.arange(N_PAIR, dtype=jnp.int32))
    return result.reshape(N_PAIR * ROWB * TILE, JCOL)
```

```python
import functools
import jax
import jax.numpy as jnp
from jax import lax
from jax.experimental import pallas as pl
from jax.experimental.pallas import tpu as pltpu
from jax.sharding import PartitionSpec as P

REACH = 2
WINDOW = 2 * REACH + 1
CAP = 16
CANDS = WINDOW * CAP
LANES = 128
CHUNKS = 4
MESH = pl.DeviceIdType.MESH
PEERS = (4, 3, 1, 0)


def kernel(n_pair, n_virt, row_count, k_count, idx_ref, tag_ref, amp_hbm, int_hbm, out_ref,
           amps_recv, ints, pack, pref, assembled, tags_in, order, order_s, own, xsend, xrecv,
           amp_sem, int_sem, order_sem, tag_send, tag_recv, tile_send, tile_recv, x_send, x_recv):
    p = lax.axis_index("pair")
    v = lax.axis_index("virt")
    amps, recv = amps_recv
    rows, edge = recv[0].shape[1:]
    cols = out_ref.shape[1]
    pair_of = [lax.rem(p + o - REACH + n_pair, n_pair) for o in range(WINDOW)]
    virt_of = [lax.rem(v + t, n_virt) for t in range(n_virt)]

    barrier = pltpu.get_barrier_semaphore()
    for o in PEERS:
        pl.semaphore_signal(barrier, inc=1, device_id=(pair_of[o], v), device_id_type=MESH)
    for t in range(1, n_virt):
        pl.semaphore_signal(barrier, inc=1, device_id=(p, virt_of[t]), device_id_type=MESH)

    amp_copies = []
    for j in range(CHUNKS):
        c = pltpu.make_async_copy(amp_hbm.at[0, 0, :, pl.ds(j * rows, rows), :], amps[j], amp_sem.at[j])
        c.start()
        amp_copies.append(c)
    send_order = (2, 1, 3, 0)
    int_copies = {}
    for t in send_order:
        start = pl.multiple_of(virt_of[t] * cols, cols)
        c = pltpu.make_async_copy(int_hbm.at[0, :, pl.ds(start, cols)], ints.at[t], int_sem.at[t])
        c.start()
        int_copies[t] = c

    def pack_chunk(j):
        for o in PEERS + (REACH,):
            def body(s, _, o=o):
                tile = amps[j][jnp.clip(idx_ref[o * CAP + s], 0, amps[j].shape[0] - 1)]
                if o == REACH:
                    recv[j][o * CAP + s] = tile
                else:
                    pack[j, o, s] = tile
                return 0
            lax.fori_loop(0, CAP, body, 0, unroll=True)

    tile_copies = {}

    def send_chunk(j):
        for o in PEERS:
            c = pltpu.make_async_remote_copy(
                src_ref=pack.at[j, o], dst_ref=recv[j].at[pl.ds(o * CAP, CAP)],
                send_sem=tile_send.at[j, o], recv_sem=tile_recv.at[j, o],
                device_id=(pair_of[o], v), device_id_type=MESH)
            c.start()
            tile_copies[j, o] = c

    amp_copies[0].wait()
    pack_chunk(0)
    pl.semaphore_wait(barrier, len(PEERS) + n_virt - 1)
    tag_copies = []
    for o in PEERS:
        c = pltpu.make_async_remote_copy(
            src_ref=tag_ref, dst_ref=tags_in.at[o], send_sem=tag_send.at[o], recv_sem=tag_recv.at[o],
            device_id=(pair_of[o], v), device_id_type=MESH)
        c.start()
        tag_copies.append(c)
    send_chunk(0)
    for j in range(1, CHUNKS):
        amp_copies[j].wait()
        pack_chunk(j)
        send_chunk(j)

    for c in tag_copies:
        c.wait()
    lane8 = lax.broadcasted_iota(jnp.int32, (8, LANES), 1)
    tag8 = jnp.full((8, LANES), row_count * k_count, jnp.int32)
    for o in range(WINDOW):
        got = tag_ref[...] if o == REACH else tags_in[o]
        tag8 = jnp.where((lane8 >= o * CAP) & (lane8 < (o + 1) * CAP), got, tag8)
    lane = lax.broadcasted_iota(jnp.int32, (LANES, LANES), 1).astype(jnp.float32)
    sub = lax.broadcasted_iota(jnp.int32, (LANES, LANES), 0).astype(jnp.float32)
    tag_r = jnp.broadcast_to(tag8[0:1, :].astype(jnp.float32), (LANES, LANES))
    tag_c = tag_r.T
    key_r = tag_r * LANES + lane
    key_c = tag_c * LANES + sub
    rank_c = jnp.sum(jnp.where(key_r < key_c, 1.0, 0.0), axis=1, keepdims=True)
    again_c = jnp.max(jnp.where((tag_r == tag_c) & (lane < sub), 1.0, 0.0), axis=1, keepdims=True)
    here = jnp.where(rank_c == lane, 1.0, 0.0)
    perm = jnp.sum(here * sub, axis=0, keepdims=True)
    again = jnp.sum(here * again_c, axis=0, keepdims=True)
    upto = jnp.sum(jnp.where(tag_c <= lane, 1.0, 0.0), axis=0, keepdims=True)
    equal = jnp.sum(jnp.where(tag_c == lane, 1.0, 0.0), axis=0, keepdims=True)
    last = jnp.where(equal > 0, upto - 1.0, float(CANDS))
    order[...] = jnp.zeros_like(order)
    order[0:1, :] = perm.astype(jnp.int32)
    order[1:2, :] = again.astype(jnp.int32)
    order[2:3, :] = last.astype(jnp.int32)
    to_scalar = pltpu.make_async_copy(order, order_s, order_sem)
    to_scalar.start()
    pref[CANDS] = jnp.zeros_like(pref[CANDS])
    to_scalar.wait()

    x_copies = {}

    def finish(j):
        for t in range(1, n_virt):
            x_copies[j, t].wait()
        total = own[j % 2]
        for t in range(1, n_virt):
            total = total + xrecv[j, t].astype(jnp.float32)
        for r in range(row_count):
            out_ref[pl.ds(r * edge + j * rows, rows), :] = total[r * rows:(r + 1) * rows]

    for j in range(CHUNKS):
        for o in PEERS:
            tile_copies[j, o].wait()

        def add(i, acc, j=j):
            for u in range(8):
                at = i * 8 + u
                tile = recv[j][jnp.clip(order_s[0, at], 0, CANDS - 1)].astype(jnp.float32)
                acc = acc * order_s[1, at].astype(jnp.float32) + tile
                pref[at] = acc.astype(jnp.bfloat16)
            return acc

        lax.fori_loop(0, CANDS // 8, add, jnp.zeros((rows, LANES), jnp.float32))
        for r in range(row_count):
            for k in range(k_count):
                assembled[pl.ds(r * rows, rows), pl.ds(k * LANES, LANES)] = pref[jnp.clip(order_s[2, r * k_count + k], 0, CANDS)]
        for t in send_order:
            if j == 0:
                int_copies[t].wait()
            part = jnp.dot(assembled[...], ints[t], preferred_element_type=jnp.float32)
            if t == 0:
                own[j % 2] = part
            else:
                xsend[j, t] = part.astype(jnp.bfloat16)
                c = pltpu.make_async_remote_copy(
                    src_ref=xsend.at[j, t], dst_ref=xrecv.at[j, t], send_sem=x_send.at[j, t], recv_sem=x_recv.at[j, t],
                    device_id=(p, virt_of[t]), device_id_type=MESH)
                c.start()
                x_copies[j, t] = c
        if j > 0:
            finish(j - 1)
    finish(CHUNKS - 1)


def on_device(n_pair, n_virt, amplitudes, offsets, row_blocks, k_blocks, screen, integrals, row_gaps, col_gaps):
    slots, edge = amplitudes.shape[2], amplitudes.shape[3]
    k_count = integrals.shape[1] // edge
    row_count = row_gaps.shape[0] // edge
    cols = col_gaps.shape[0]
    rows = edge // CHUNKS
    off, blk = offsets[0, 0, :, 0], row_blocks[0, 0] * k_count + k_blocks[0, 0]
    wanted = jnp.where(screen[0, 0] == 1, off, -1)
    slot = jnp.arange(slots, dtype=jnp.int32)
    earlier = (wanted[:, None] == wanted[None, :]) & (slot[:, None] < slot[None, :])
    rank = jnp.sum(earlier.astype(jnp.int32), axis=0)
    place = jnp.where(wanted < 0, -1, wanted * CAP + rank)
    lane = jnp.arange(LANES, dtype=jnp.int32)
    hit = place[None, :] == lane[:, None]
    idx = jnp.sum(jnp.where(hit, slot[None, :], 0), axis=1)
    none = row_count * k_count
    tag = none + jnp.sum(jnp.where(hit, blk[None, :] - none, 0), axis=1)
    tag = jnp.broadcast_to(tag[None, :], (8, LANES))

    cycle = pl.pallas_call(
        functools.partial(kernel, n_pair, n_virt, row_count, k_count),
        out_shape=jax.ShapeDtypeStruct((row_count * edge, cols), jnp.float32),
        in_specs=[
            pl.BlockSpec(memory_space=pltpu.SMEM),
            pl.BlockSpec(memory_space=pltpu.VMEM),
            pl.BlockSpec(memory_space=pl.ANY),
            pl.BlockSpec(memory_space=pl.ANY),
        ],
        out_specs=pl.BlockSpec(memory_space=pltpu.VMEM),
        scratch_shapes=[
            ([pltpu.VMEM((slots, rows, edge), jnp.bfloat16)] * CHUNKS, [pltpu.VMEM((CANDS, rows, edge), jnp.bfloat16)] * CHUNKS),
            pltpu.VMEM((n_virt, k_count * edge, cols), jnp.bfloat16),
            pltpu.VMEM((CHUNKS, WINDOW, CAP, rows, edge), jnp.bfloat16),
            pltpu.VMEM((CANDS + 1, rows, edge), jnp.bfloat16),
            pltpu.VMEM((row_count * rows, k_count * edge), jnp.bfloat16),
            pltpu.VMEM((WINDOW, 8, LANES), jnp.int32),
            pltpu.VMEM((8, LANES), jnp.int32),
            pltpu.SMEM((8, LANES), jnp.int32),
            pltpu.VMEM((2, row_count * rows, cols), jnp.float32),
            pltpu.VMEM((CHUNKS, n_virt, row_count * rows, cols), jnp.bfloat16),
            pltpu.VMEM((CHUNKS, n_virt, row_count * rows, cols), jnp.bfloat16),
            pltpu.SemaphoreType.DMA((CHUNKS,)),
            pltpu.SemaphoreType.DMA((n_virt,)),
            pltpu.SemaphoreType.DMA,
            pltpu.SemaphoreType.DMA((WINDOW,)),
            pltpu.SemaphoreType.DMA((WINDOW,)),
            pltpu.SemaphoreType.DMA((CHUNKS, WINDOW)),
            pltpu.SemaphoreType.DMA((CHUNKS, WINDOW)),
            pltpu.SemaphoreType.DMA((CHUNKS, n_virt)),
            pltpu.SemaphoreType.DMA((CHUNKS, n_virt)),
        ],
        compiler_params=pltpu.CompilerParams(
            collective_id=0, has_side_effects=True, vmem_limit_bytes=60 * 1024 * 1024),
        name="cycle",
    )(idx, tag, amplitudes, integrals)
    return cycle / (row_gaps[:, None] + col_gaps[None, :])


def solution(mesh):
    return jax.shard_map(
        functools.partial(on_device, mesh.shape["pair"], mesh.shape["virt"]),
        mesh=mesh,
        in_specs=(
            P("pair", "virt", None, None, None),
            P("pair", "virt", None, None),
            P("pair", "virt", None),
            P("pair", "virt", None),
            P("pair", "virt", None),
            P("pair", "virt", None),
            P("pair"),
            P("virt"),
        ),
        out_specs=P("pair", "virt"),
        check_vma=False,
    )
```

```python
import functools
import jax
import jax.numpy as jnp
from jax import lax
from jax.experimental import pallas as pl
from jax.experimental.pallas import tpu as pltpu
from jax.sharding import PartitionSpec as P

REACH = 2
WINDOW = 2 * REACH + 1
CAP = 16
CANDS = WINDOW * CAP
LANES = 128
SIZES = (32, 32, 32, 16, 16)
STARTS = tuple(sum(SIZES[:j]) for j in range(len(SIZES)))
CHUNKS = len(SIZES)
AHEAD = 3
LAG = 2
MESH = pl.DeviceIdType.MESH
PEERS = (4, 3, 1, 0)


def kernel(n_pair, n_virt, row_count, k_count, off_hbm, row_hbm, kb_hbm, screen_hbm, amp_hbm, int_hbm, rgap_hbm, cgap_hbm, out_ref,
           amps, pack, recv, pref, assembled, own, xsend, xrecv, ints, tags_in, tag_own, rowbuf, small, rgap, cgap, rowmat, order, idx_s, order_s,
           amp_sem, int_sem, small_sem, gap_sem, idx_sem, order_sem, tag_send, tag_recv, tile_send, tile_recv, x_send, x_recv):
    p = lax.axis_index("pair")
    v = lax.axis_index("virt")
    slots, edge = amp_hbm.shape[2:4]
    cols = out_ref.shape[1]
    pair_of = [lax.rem(p + o - REACH + n_pair, n_pair) for o in range(WINDOW)]
    virt_of = [lax.rem(v + t, n_virt) for t in range(n_virt)]

    small_copies = []
    for i, ref in enumerate((off_hbm, row_hbm, kb_hbm, screen_hbm)):
        c = pltpu.make_async_copy(ref.at[0], small.at[i], small_sem.at[i])
        c.start()
        small_copies.append(c)
    barrier = pltpu.get_barrier_semaphore()
    for o in PEERS:
        pl.semaphore_signal(barrier, inc=1, device_id=(pair_of[o], v), device_id_type=MESH)
    for t in range(1, n_virt):
        pl.semaphore_signal(barrier, inc=1, device_id=(p, virt_of[t]), device_id_type=MESH)

    amp_copies = []
    for j in range(CHUNKS):
        c = pltpu.make_async_copy(amp_hbm.at[0, 0, :, pl.ds(STARTS[j], SIZES[j]), :], amps[j], amp_sem.at[j])
        c.start()
        amp_copies.append(c)
    send_order = (2, 1, 3, 0)
    int_copies = {}
    for t in send_order:
        start = pl.multiple_of(virt_of[t] * cols, cols)
        c = pltpu.make_async_copy(int_hbm.at[0, :, pl.ds(start, cols)], ints.at[t], int_sem.at[t])
        c.start()
        int_copies[t] = c

    gap_copies = [pltpu.make_async_copy(rgap_hbm, rgap, gap_sem.at[0]), pltpu.make_async_copy(cgap_hbm, cgap, gap_sem.at[1])]
    for c in gap_copies:
        c.start()

    none = float(row_count * k_count)
    lane = lax.broadcasted_iota(jnp.int32, (LANES, LANES), 1).astype(jnp.float32)
    sub = lax.broadcasted_iota(jnp.int32, (LANES, LANES), 0).astype(jnp.float32)
    for c in small_copies:
        c.wait()
    rowbuf[...] = jnp.full(rowbuf.shape, -1.0, jnp.float32)
    rowbuf[0:1, 0:slots] = jnp.where(small[3] == 1, small[0], -1).astype(jnp.float32)
    rowbuf[1:2, 0:slots] = (small[1] * k_count + small[2]).astype(jnp.float32)
    want_r = jnp.broadcast_to(rowbuf[0:1, :], (LANES, LANES))
    want_c = want_r.T[:slots]
    blk_c = jnp.broadcast_to(rowbuf[1:2, :], (LANES, LANES)).T[:slots]
    lane_s, sub_s = lane[:slots], sub[:slots]
    rank = jnp.sum(jnp.where((want_r[:slots] == want_c) & (lane_s < sub_s), 1.0, 0.0), axis=1, keepdims=True)
    place = jnp.where(want_c < 0, -1.0, want_c * CAP + rank)
    hit = jnp.where(place == lane_s, 1.0, 0.0)
    slot_of = jnp.sum(hit * sub_s, axis=0, keepdims=True)
    tag_of = none + jnp.sum(hit * (blk_c - none), axis=0, keepdims=True)
    order[0] = jnp.broadcast_to(slot_of.astype(jnp.int32), (8, LANES))
    to_idx = pltpu.make_async_copy(order.at[0], idx_s, idx_sem)
    to_idx.start()
    tag_own[...] = jnp.broadcast_to(tag_of, (8, LANES))
    to_idx.wait()

    def pack_tiles(j, o):
        for s in range(CAP):
            tile = amps[j][jnp.clip(idx_s[0, o * CAP + s], 0, slots - 1)]
            if o == REACH:
                recv[j][o * CAP + s] = tile
            else:
                pack[j][o, s] = tile

    tile_copies = {}

    def send_tiles(j, o):
        c = pltpu.make_async_remote_copy(
            src_ref=pack[j].at[o], dst_ref=recv[j].at[pl.ds(o * CAP, CAP)],
            send_sem=tile_send.at[j, o], recv_sem=tile_recv.at[j, o],
            device_id=(pair_of[o], v), device_id_type=MESH)
        c.start()
        tile_copies[j, o] = c

    amp_copies[0].wait()
    pack_tiles(0, PEERS[0])
    pl.semaphore_wait(barrier, len(PEERS) + n_virt - 1)
    send_tiles(0, PEERS[0])
    for o in PEERS[1:]:
        pack_tiles(0, o)
        send_tiles(0, o)
    tag_copies = []
    for o in PEERS:
        c = pltpu.make_async_remote_copy(
            src_ref=tag_own, dst_ref=tags_in.at[o], send_sem=tag_send.at[o], recv_sem=tag_recv.at[o],
            device_id=(pair_of[o], v), device_id_type=MESH)
        c.start()
        tag_copies.append(c)
    pack_tiles(0, REACH)
    for j in range(1, CHUNKS):
        amp_copies[j].wait()
        for o in PEERS:
            pack_tiles(j, o)
            if j < AHEAD:
                send_tiles(j, o)
        pack_tiles(j, REACH)

    for c in tag_copies:
        c.wait()
    lane8 = lane[:8]
    tag8 = jnp.full((8, LANES), none, jnp.float32)
    for o in range(WINDOW):
        got = tag_own[...] if o == REACH else tags_in[o]
        tag8 = jnp.where((lane8 >= o * CAP) & (lane8 < (o + 1) * CAP), got, tag8)
    tag_r = jnp.broadcast_to(tag8[0:1, :], (LANES, LANES))
    tag_c = tag_r.T
    key_r = tag_r * LANES + lane
    key_c = tag_c * LANES + sub
    rank_c = jnp.sum(jnp.where(key_r < key_c, 1.0, 0.0), axis=1, keepdims=True)
    again_c = jnp.max(jnp.where((tag_r == tag_c) & (lane < sub), 1.0, 0.0), axis=1, keepdims=True)
    here = jnp.where(rank_c == lane, 1.0, 0.0)
    perm = jnp.sum(here * sub, axis=0, keepdims=True)
    again = jnp.sum(here * again_c, axis=0, keepdims=True)
    upto = jnp.sum(jnp.where(tag_c <= lane, 1.0, 0.0), axis=0, keepdims=True)
    equal = jnp.sum(jnp.where(tag_c == lane, 1.0, 0.0), axis=0, keepdims=True)
    last = jnp.where(equal > 0, upto - 1.0, float(CANDS))
    order[1] = jnp.zeros((8, LANES), jnp.int32)
    order[1, 0:1, :] = perm.astype(jnp.int32)
    order[1, 1:2, :] = again.astype(jnp.int32)
    order[1, 2:3, :] = last.astype(jnp.int32)
    to_order = pltpu.make_async_copy(order.at[1], order_s, order_sem)
    to_order.start()
    for c in gap_copies:
        c.wait()
    for r in range(row_count):
        gaps = rgap[pl.ds(r * edge, edge)].reshape(1, edge)
        rowmat[pl.ds(r * edge, edge), :] = jnp.broadcast_to(gaps, (edge, LANES)).T
    for j in range(CHUNKS):
        pref[j][CANDS] = jnp.zeros(pref[j].shape[1:], jnp.bfloat16)
    to_order.wait()

    x_copies = {}

    def finish(j):
        for t in range(1, n_virt):
            x_copies[j, t].wait()
        total = own[j][...]
        for t in range(1, n_virt):
            total = total + xrecv[j][t].astype(jnp.float32)
        rows, col_gap = SIZES[j], cgap[...].reshape(1, cols)
        for r in range(row_count):
            row_gap = rowmat[pl.ds(r * edge + STARTS[j], rows), :]
            gap = jnp.concatenate([row_gap] * (cols // LANES), axis=1) + col_gap
            out_ref[pl.ds(r * edge + STARTS[j], rows), :] = total[r * rows:(r + 1) * rows] / gap

    for j in range(CHUNKS):
        if j + AHEAD < CHUNKS:
            for o in PEERS:
                tile_copies[j, o].wait_send()
            for o in PEERS:
                send_tiles(j + AHEAD, o)
        for o in PEERS:
            tile_copies[j, o].wait_recv()
        rows = SIZES[j]

        acc = jnp.zeros((rows, LANES), jnp.float32)
        for at in range(CANDS):
            tile = recv[j][jnp.clip(order_s[0, at], 0, CANDS - 1)].astype(jnp.float32)
            acc = jnp.where(order_s[1, at] > 0, acc, 0.0) + tile
            pref[j][at] = acc.astype(jnp.bfloat16)
        for r in range(row_count):
            for k in range(k_count):
                block = pref[j][jnp.clip(order_s[2, r * k_count + k], 0, CANDS)]
                assembled[j][pl.ds(r * rows, rows), pl.ds(k * LANES, LANES)] = block
        for t in send_order:
            if j == 0:
                int_copies[t].wait()
            part = jnp.dot(assembled[j][...], ints[t], preferred_element_type=jnp.float32)
            if t == 0:
                own[j][...] = part
            else:
                xsend[j][t] = part.astype(jnp.bfloat16)
                c = pltpu.make_async_remote_copy(
                    src_ref=xsend[j].at[t], dst_ref=xrecv[j].at[t], send_sem=x_send.at[j, t], recv_sem=x_recv.at[j, t],
                    device_id=(p, virt_of[t]), device_id_type=MESH)
                c.start()
                x_copies[j, t] = c
        if j >= LAG:
            finish(j - LAG)
    for j in range(max(0, CHUNKS - AHEAD), CHUNKS):
        for o in PEERS:
            tile_copies[j, o].wait_send()
    for j in range(max(0, CHUNKS - LAG), CHUNKS):
        finish(j)


def on_device(n_pair, n_virt, amplitudes, offsets, row_blocks, k_blocks, screen, integrals, row_gaps, col_gaps):
    slots, edge = amplitudes.shape[2], amplitudes.shape[3]
    k_count = integrals.shape[1] // edge
    row_count = row_gaps.shape[0] // edge
    cols = col_gaps.shape[0]

    def chunked(shape_of, dtype):
        return [pltpu.VMEM(shape_of(rows), dtype) for rows in SIZES]

    operands = (offsets[..., 0], row_blocks, k_blocks, screen, amplitudes, integrals, row_gaps, col_gaps)
    return pl.pallas_call(
        functools.partial(kernel, n_pair, n_virt, row_count, k_count),
        out_shape=jax.ShapeDtypeStruct((row_count * edge, cols), jnp.float32),
        in_specs=[pl.BlockSpec(memory_space=pltpu.HBM)] * 8,
        out_specs=pl.BlockSpec(memory_space=pltpu.VMEM),
        scratch_shapes=[
            chunked(lambda rows: (slots, rows, edge), jnp.bfloat16),
            chunked(lambda rows: (WINDOW, CAP, rows, edge), jnp.bfloat16),
            chunked(lambda rows: (CANDS, rows, edge), jnp.bfloat16),
            chunked(lambda rows: (CANDS + 1, rows, edge), jnp.bfloat16),
            chunked(lambda rows: (row_count * rows, k_count * edge), jnp.bfloat16),
            chunked(lambda rows: (row_count * rows, cols), jnp.float32),
            chunked(lambda rows: (n_virt, row_count * rows, cols), jnp.bfloat16),
            chunked(lambda rows: (n_virt, row_count * rows, cols), jnp.bfloat16),
            pltpu.VMEM((n_virt, k_count * edge, cols), jnp.bfloat16),
            pltpu.VMEM((WINDOW, 8, LANES), jnp.float32),
            pltpu.VMEM((8, LANES), jnp.float32),
            pltpu.VMEM((8, LANES), jnp.float32),
            pltpu.VMEM((4, 1, slots), jnp.int32),
            pltpu.VMEM((row_count * edge,), jnp.float32),
            pltpu.VMEM((cols,), jnp.float32),
            pltpu.VMEM((row_count * edge, LANES), jnp.float32),
            pltpu.VMEM((2, 8, LANES), jnp.int32),
            pltpu.SMEM((8, LANES), jnp.int32),
            pltpu.SMEM((8, LANES), jnp.int32),
            pltpu.SemaphoreType.DMA((CHUNKS,)),
            pltpu.SemaphoreType.DMA((n_virt,)),
            pltpu.SemaphoreType.DMA((4,)),
            pltpu.SemaphoreType.DMA((2,)),
            pltpu.SemaphoreType.DMA,
            pltpu.SemaphoreType.DMA,
            pltpu.SemaphoreType.DMA((WINDOW,)),
            pltpu.SemaphoreType.DMA((WINDOW,)),
            pltpu.SemaphoreType.DMA((CHUNKS, WINDOW)),
            pltpu.SemaphoreType.DMA((CHUNKS, WINDOW)),
            pltpu.SemaphoreType.DMA((CHUNKS, n_virt)),
            pltpu.SemaphoreType.DMA((CHUNKS, n_virt)),
        ],
        compiler_params=pltpu.CompilerParams(
            collective_id=0, has_side_effects=True, vmem_limit_bytes=40 * 1024 * 1024),
        name="cycle",
    )(*[pltpu.with_memory_space_constraint(x, pltpu.HBM) for x in operands])


def solution(mesh):
    return jax.shard_map(
        functools.partial(on_device, mesh.shape["pair"], mesh.shape["virt"]),
        mesh=mesh,
        in_specs=(
            P("pair", "virt", None, None, None),
            P("pair", "virt", None, None),
            P("pair", "virt", None),
            P("pair", "virt", None),
            P("pair", "virt", None),
            P("pair", "virt", None),
            P("pair"),
            P("virt"),
        ),
        out_specs=P("pair", "virt"),
        check_vma=False,
    )
```

```python
import functools
import jax
import jax.numpy as jnp
from jax import lax
from jax.experimental import pallas as pl
from jax.experimental.pallas import tpu as pltpu
from jax.sharding import PartitionSpec as P

REACH = 2
WINDOW = 2 * REACH + 1
CAP = 16
CANDS = WINDOW * CAP
LANES = 128
SIZES = (32, 32, 32, 16, 16)
STARTS = tuple(sum(SIZES[:j]) for j in range(len(SIZES)))
CHUNKS = len(SIZES)
AHEAD = 3
LAG = 2
MESH = pl.DeviceIdType.MESH
PEERS = (4, 3, 1, 0)
REMOTE = (WINDOW - 1) * CAP


def place_of(o):
    return WINDOW - 1 if o == REACH else o - (o > REACH)


def wait_bytes(ref, sem):
    pltpu.make_async_copy(ref, ref, sem).wait()


def kernel(n_pair, n_virt, row_count, k_count, off_hbm, row_hbm, kb_hbm, screen_hbm, amp_hbm, int_hbm, rgap_hbm, cgap_hbm, out_ref,
           amp_first, amp_rest, pack, recv, pref, assembled, own, xsend, xrecv, ints, tags_in, tag_own, rowbuf, small, rgap, cgap, rowmat, order, idx_s, order_s,
           amp_sem, int_sem, small_sem, gap_sem, order_sem, tag_send, tag_recv, tile_send, tile_recv, x_send, x_recv):
    p = lax.axis_index("pair")
    v = lax.axis_index("virt")
    slots, edge = amp_hbm.shape[2:4]
    cols = out_ref.shape[1]
    pair_of = [lax.rem(p + o - REACH + n_pair, n_pair) for o in range(WINDOW)]
    virt_of = [lax.rem(v + t, n_virt) for t in range(n_virt)]

    small_copies = []
    for i, ref in enumerate((off_hbm, row_hbm, kb_hbm, screen_hbm)):
        c = pltpu.make_async_copy(ref.at[0], small.at[i], small_sem.at[i])
        c.start()
        small_copies.append(c)
    barrier = pltpu.get_barrier_semaphore()
    for o in PEERS:
        pl.semaphore_signal(barrier, inc=1, device_id=(pair_of[o], v), device_id_type=MESH)
    for t in range(1, n_virt):
        pl.semaphore_signal(barrier, inc=1, device_id=(p, virt_of[t]), device_id_type=MESH)

    first = SIZES[0]
    amp_copies = [
        pltpu.make_async_copy(amp_hbm.at[0, 0, :, pl.ds(0, first), :], amp_first, amp_sem.at[0]),
        pltpu.make_async_copy(amp_hbm.at[0, 0, :, pl.ds(first, edge - first), :], amp_rest, amp_sem.at[1]),
    ]
    int_copy = pltpu.make_async_copy(int_hbm.at[0], ints, int_sem)
    for c in amp_copies:
        c.start()
    int_copy.start()
    gap_copies = [pltpu.make_async_copy(rgap_hbm, rgap, gap_sem.at[0]), pltpu.make_async_copy(cgap_hbm, cgap, gap_sem.at[1])]
    for c in gap_copies:
        c.start()

    none = float(row_count * k_count)
    lane = lax.broadcasted_iota(jnp.int32, (LANES, LANES), 1).astype(jnp.float32)
    sub = lax.broadcasted_iota(jnp.int32, (LANES, LANES), 0).astype(jnp.float32)
    for c in small_copies:
        c.wait()
    rowbuf[...] = jnp.full(rowbuf.shape, -1.0, jnp.float32)
    rowbuf[0:1, 0:slots] = jnp.where(small[3] == 1, small[0], -1).astype(jnp.float32)
    rowbuf[1:2, 0:slots] = (small[1] * k_count + small[2]).astype(jnp.float32)
    want_r = jnp.broadcast_to(rowbuf[0:1, :], (LANES, LANES))
    want_c = want_r.T[:slots]
    blk_c = jnp.broadcast_to(rowbuf[1:2, :], (LANES, LANES)).T[:slots]
    lane_s, sub_s = lane[:slots], sub[:slots]
    rank = jnp.sum(jnp.where((want_r[:slots] == want_c) & (lane_s < sub_s), 1.0, 0.0), axis=1, keepdims=True)
    position = jnp.where(want_c > REACH, want_c - 1, jnp.where(want_c == REACH, float(WINDOW - 1), want_c))
    place = jnp.where(want_c < 0, -1.0, position * CAP + rank)
    hit = jnp.where(place == lane_s, 1.0, 0.0)
    slot_of = jnp.sum(hit * sub_s, axis=0, keepdims=True)
    tag_of = none + jnp.sum(hit * (blk_c - none), axis=0, keepdims=True)
    order[0] = jnp.broadcast_to(slot_of.astype(jnp.int32), (8, LANES))
    to_idx = pltpu.make_async_copy(order.at[0], idx_s, order_sem)
    to_idx.start()
    tag_own[...] = jnp.broadcast_to(tag_of, (8, LANES))
    to_idx.wait()

    def pack_tiles(j, o):
        for s in range(CAP):
            slot = jnp.clip(idx_s[0, place_of(o) * CAP + s], 0, slots - 1)
            tile = amp_first[slot] if j == 0 else amp_rest[slot, pl.ds(STARTS[j] - first, SIZES[j]), :]
            if o == REACH:
                recv[j][REMOTE + s] = tile
            else:
                pack[j][place_of(o) * CAP + s] = tile

    def send_tiles(j, o):
        there = pl.ds(place_of(o) * CAP, CAP)
        pltpu.make_async_remote_copy(
            src_ref=pack[j].at[there], dst_ref=recv[j].at[there], send_sem=tile_send.at[j], recv_sem=tile_recv.at[j],
            device_id=(pair_of[o], v), device_id_type=MESH).start()

    amp_copies[0].wait()
    pack_tiles(0, PEERS[0])
    pl.semaphore_wait(barrier, len(PEERS) + n_virt - 1)
    send_tiles(0, PEERS[0])
    for o in PEERS[1:]:
        pack_tiles(0, o)
        send_tiles(0, o)
    for o in PEERS:
        pltpu.make_async_remote_copy(
            src_ref=tag_own, dst_ref=tags_in.at[place_of(o)], send_sem=tag_send, recv_sem=tag_recv,
            device_id=(pair_of[o], v), device_id_type=MESH).start()
    pack_tiles(0, REACH)
    amp_copies[1].wait()
    for j in range(1, CHUNKS):
        for o in PEERS:
            pack_tiles(j, o)
            if j < AHEAD:
                send_tiles(j, o)
        pack_tiles(j, REACH)

    wait_bytes(tags_in, tag_recv)
    wait_bytes(tags_in, tag_send)
    lane8 = lane[:8]
    tag8 = jnp.full((8, LANES), none, jnp.float32)
    for o in range(WINDOW):
        got = tag_own[...] if o == WINDOW - 1 else tags_in[o]
        tag8 = jnp.where((lane8 >= o * CAP) & (lane8 < (o + 1) * CAP), got, tag8)
    tag_r = jnp.broadcast_to(tag8[0:1, :], (LANES, LANES))
    tag_c = tag_r.T
    key_r = tag_r * LANES + lane
    key_c = tag_c * LANES + sub
    rank_c = jnp.sum(jnp.where(key_r < key_c, 1.0, 0.0), axis=1, keepdims=True)
    again_c = jnp.max(jnp.where((tag_r == tag_c) & (lane < sub), 1.0, 0.0), axis=1, keepdims=True)
    here = jnp.where(rank_c == lane, 1.0, 0.0)
    perm = jnp.sum(here * sub, axis=0, keepdims=True)
    again = jnp.sum(here * again_c, axis=0, keepdims=True)
    upto = jnp.sum(jnp.where(tag_c <= lane, 1.0, 0.0), axis=0, keepdims=True)
    equal = jnp.sum(jnp.where(tag_c == lane, 1.0, 0.0), axis=0, keepdims=True)
    last = jnp.where(equal > 0, upto - 1.0, float(CANDS))
    order[1] = jnp.zeros((8, LANES), jnp.int32)
    order[1, 0:1, :] = perm.astype(jnp.int32)
    order[1, 1:2, :] = again.astype(jnp.int32)
    order[1, 2:3, :] = last.astype(jnp.int32)
    to_order = pltpu.make_async_copy(order.at[1], order_s, order_sem)
    to_order.start()
    for c in gap_copies:
        c.wait()
    for r in range(row_count):
        gaps = rgap[pl.ds(r * edge, edge)].reshape(1, edge)
        rowmat[pl.ds(r * edge, edge), :] = jnp.broadcast_to(gaps, (edge, LANES)).T
    for j in range(CHUNKS):
        pref[j][CANDS] = jnp.zeros(pref[j].shape[1:], jnp.bfloat16)
    to_order.wait()

    def finish(j):
        wait_bytes(xsend[j], x_send.at[j])
        wait_bytes(xrecv[j], x_recv.at[j])
        total = own[j][...]
        for t in range(1, n_virt):
            total = total + xrecv[j][t - 1].astype(jnp.float32)
        rows, col_gap = SIZES[j], cgap[...].reshape(1, cols)
        for r in range(row_count):
            row_gap = rowmat[pl.ds(r * edge + STARTS[j], rows), :]
            gap = jnp.concatenate([row_gap] * (cols // LANES), axis=1) + col_gap
            out_ref[pl.ds(r * edge + STARTS[j], rows), :] = total[r * rows:(r + 1) * rows] / gap

    send_order = (2, 1, 3, 0)
    for j in range(CHUNKS):
        if j + AHEAD < CHUNKS:
            wait_bytes(pack[j], tile_send.at[j])
            for o in PEERS:
                send_tiles(j + AHEAD, o)
        wait_bytes(recv[j].at[pl.ds(0, REMOTE)], tile_recv.at[j])
        rows = SIZES[j]

        acc = jnp.zeros((rows, LANES), jnp.float32)
        for at in range(CANDS):
            tile = recv[j][jnp.clip(order_s[0, at], 0, CANDS - 1)].astype(jnp.float32)
            acc = jnp.where(order_s[1, at] > 0, acc, 0.0) + tile
            pref[j][at] = acc.astype(jnp.bfloat16)
        for r in range(row_count):
            for k in range(k_count):
                block = pref[j][jnp.clip(order_s[2, r * k_count + k], 0, CANDS)]
                assembled[j][pl.ds(r * rows, rows), pl.ds(k * LANES, LANES)] = block
        for t in send_order:
            if j == 0 and t == send_order[0]:
                int_copy.wait()
            columns = pl.ds(pl.multiple_of(virt_of[t] * cols, cols), cols)
            part = jnp.dot(assembled[j][...], ints[:, columns], preferred_element_type=jnp.float32)
            if t == 0:
                own[j][...] = part
            else:
                xsend[j][t - 1] = part.astype(jnp.bfloat16)
                pltpu.make_async_remote_copy(
                    src_ref=xsend[j].at[t - 1], dst_ref=xrecv[j].at[t - 1], send_sem=x_send.at[j], recv_sem=x_recv.at[j],
                    device_id=(p, virt_of[t]), device_id_type=MESH).start()
        if j >= LAG:
            finish(j - LAG)
    for j in range(max(0, CHUNKS - AHEAD), CHUNKS):
        wait_bytes(pack[j], tile_send.at[j])
    for j in range(max(0, CHUNKS - LAG), CHUNKS):
        finish(j)


def on_device(n_pair, n_virt, amplitudes, offsets, row_blocks, k_blocks, screen, integrals, row_gaps, col_gaps):
    slots, edge = amplitudes.shape[2], amplitudes.shape[3]
    k_count = integrals.shape[1] // edge
    row_count = row_gaps.shape[0] // edge
    cols = col_gaps.shape[0]

    def chunked(shape_of, dtype):
        return [pltpu.VMEM(shape_of(rows), dtype) for rows in SIZES]

    operands = (offsets[..., 0], row_blocks, k_blocks, screen, amplitudes, integrals, row_gaps, col_gaps)
    return pl.pallas_call(
        functools.partial(kernel, n_pair, n_virt, row_count, k_count),
        out_shape=jax.ShapeDtypeStruct((row_count * edge, cols), jnp.float32),
        in_specs=[pl.BlockSpec(memory_space=pltpu.HBM)] * 8,
        out_specs=pl.BlockSpec(memory_space=pltpu.VMEM),
        scratch_shapes=[
            pltpu.VMEM((slots, SIZES[0], edge), jnp.bfloat16),
            pltpu.VMEM((slots, edge - SIZES[0], edge), jnp.bfloat16),
            chunked(lambda rows: (REMOTE, rows, edge), jnp.bfloat16),
            chunked(lambda rows: (CANDS, rows, edge), jnp.bfloat16),
            chunked(lambda rows: (CANDS + 1, rows, edge), jnp.bfloat16),
            chunked(lambda rows: (row_count * rows, k_count * edge), jnp.bfloat16),
            chunked(lambda rows: (row_count * rows, cols), jnp.float32),
            chunked(lambda rows: (n_virt - 1, row_count * rows, cols), jnp.bfloat16),
            chunked(lambda rows: (n_virt - 1, row_count * rows, cols), jnp.bfloat16),
            pltpu.VMEM((k_count * edge, n_virt * cols), jnp.bfloat16),
            pltpu.VMEM((WINDOW - 1, 8, LANES), jnp.float32),
            pltpu.VMEM((8, LANES), jnp.float32),
            pltpu.VMEM((8, LANES), jnp.float32),
            pltpu.VMEM((4, 1, slots), jnp.int32),
            pltpu.VMEM((row_count * edge,), jnp.float32),
            pltpu.VMEM((cols,), jnp.float32),
            pltpu.VMEM((row_count * edge, LANES), jnp.float32),
            pltpu.VMEM((2, 8, LANES), jnp.int32),
            pltpu.SMEM((8, LANES), jnp.int32),
            pltpu.SMEM((8, LANES), jnp.int32),
            pltpu.SemaphoreType.DMA((2,)),
            pltpu.SemaphoreType.DMA,
            pltpu.SemaphoreType.DMA((4,)),
            pltpu.SemaphoreType.DMA((2,)),
            pltpu.SemaphoreType.DMA,
            pltpu.SemaphoreType.DMA,
            pltpu.SemaphoreType.DMA,
            pltpu.SemaphoreType.DMA((CHUNKS,)),
            pltpu.SemaphoreType.DMA((CHUNKS,)),
            pltpu.SemaphoreType.DMA((CHUNKS,)),
            pltpu.SemaphoreType.DMA((CHUNKS,)),
        ],
        compiler_params=pltpu.CompilerParams(
            collective_id=0, has_side_effects=True, vmem_limit_bytes=40 * 1024 * 1024),
        name="cycle",
    )(*[pltpu.with_memory_space_constraint(x, pltpu.HBM) for x in operands])


def solution(mesh):
    return jax.shard_map(
        functools.partial(on_device, mesh.shape["pair"], mesh.shape["virt"]),
        mesh=mesh,
        in_specs=(
            P("pair", "virt", None, None, None),
            P("pair", "virt", None, None),
            P("pair", "virt", None),
            P("pair", "virt", None),
            P("pair", "virt", None),
            P("pair", "virt", None),
            P("pair"),
            P("virt"),
        ),
        out_specs=P("pair", "virt"),
        check_vma=False,
    )
```

```python
import functools
import jax
import jax.numpy as jnp
from jax import lax
from jax.experimental import pallas as pl
from jax.experimental.pallas import tpu as pltpu
from jax.sharding import PartitionSpec as P

REACH = 2
WINDOW = 2 * REACH + 1
CAP = 16
CANDS = WINDOW * CAP
LANES = 128
SIZES = (32, 32, 32, 16, 16)
STARTS = tuple(sum(SIZES[:j]) for j in range(len(SIZES)))
CHUNKS = len(SIZES)
AHEAD = 3
LAG = 2
MESH = pl.DeviceIdType.MESH
PEERS = (4, 3, 1, 0)
REMOTE = (WINDOW - 1) * CAP


def place_of(o):
    return WINDOW - 1 if o == REACH else o - (o > REACH)


def wait_bytes(ref, sem):
    pltpu.make_async_copy(ref, ref, sem).wait()


def kernel(n_pair, n_virt, row_count, k_count, off_hbm, row_hbm, kb_hbm, screen_hbm, amp_hbm, int_hbm, rgap_hbm, cgap_hbm, out_ref,
           amp_first, amp_rest, pack, recv, pref, assembled, own, xsend, xrecv, ints, tags_in, tag_own, rowbuf, small, rgap, cgap, rowmat, order, idx_s, order_s,
           amp_sem, int_sem, small_sem, gap_sem, order_sem, tag_send, tag_recv, tile_send, tile_recv, x_send, x_recv):
    p = lax.axis_index("pair")
    v = lax.axis_index("virt")
    slots, edge = amp_hbm.shape[2:4]
    cols = out_ref.shape[1]
    pair_of = [lax.rem(p + o - REACH + n_pair, n_pair) for o in range(WINDOW)]
    virt_of = [lax.rem(v + t, n_virt) for t in range(n_virt)]

    small_copies = []
    for i, ref in enumerate((off_hbm, row_hbm, kb_hbm, screen_hbm)):
        c = pltpu.make_async_copy(ref.at[0], small.at[i], small_sem.at[i])
        c.start()
        small_copies.append(c)
    barrier = pltpu.get_barrier_semaphore()
    for o in PEERS:
        pl.semaphore_signal(barrier, inc=1, device_id=(pair_of[o], v), device_id_type=MESH)
    for t in range(1, n_virt):
        pl.semaphore_signal(barrier, inc=1, device_id=(p, virt_of[t]), device_id_type=MESH)

    first = SIZES[0]
    amp_copies = [
        pltpu.make_async_copy(amp_hbm.at[0, 0, :, pl.ds(0, first), :], amp_first, amp_sem.at[0]),
        pltpu.make_async_copy(amp_hbm.at[0, 0, :, pl.ds(first, edge - first), :], amp_rest, amp_sem.at[1]),
    ]
    int_copy = pltpu.make_async_copy(int_hbm.at[0], ints, int_sem)
    amp_copies[0].start()
    gap_copies = [pltpu.make_async_copy(rgap_hbm, rgap, gap_sem.at[0]), pltpu.make_async_copy(cgap_hbm, cgap, gap_sem.at[1])]

    none = float(row_count * k_count)
    lane = lax.broadcasted_iota(jnp.int32, (LANES, LANES), 1).astype(jnp.float32)
    sub = lax.broadcasted_iota(jnp.int32, (LANES, LANES), 0).astype(jnp.float32)
    for c in small_copies:
        c.wait()
    rowbuf[...] = jnp.full(rowbuf.shape, -1.0, jnp.float32)
    rowbuf[0:1, 0:slots] = jnp.where(small[3] == 1, small[0], -1).astype(jnp.float32)
    rowbuf[1:2, 0:slots] = (small[1] * k_count + small[2]).astype(jnp.float32)
    want_r = jnp.broadcast_to(rowbuf[0:1, :], (LANES, LANES))
    want_c = want_r.T[:slots]
    blk_c = jnp.broadcast_to(rowbuf[1:2, :], (LANES, LANES)).T[:slots]
    lane_s, sub_s = lane[:slots], sub[:slots]
    rank = jnp.sum(jnp.where((want_r[:slots] == want_c) & (lane_s < sub_s), 1.0, 0.0), axis=1, keepdims=True)
    position = jnp.where(want_c > REACH, want_c - 1, jnp.where(want_c == REACH, float(WINDOW - 1), want_c))
    place = jnp.where(want_c < 0, -1.0, position * CAP + rank)
    hit = jnp.where(place == lane_s, 1.0, 0.0)
    slot_of = jnp.sum(hit * sub_s, axis=0, keepdims=True)
    order[0] = jnp.broadcast_to(slot_of.astype(jnp.int32), (8, LANES))
    to_idx = pltpu.make_async_copy(order.at[0], idx_s, order_sem)
    to_idx.start()
    tag_of = none + jnp.sum(hit * (blk_c - none), axis=0, keepdims=True)
    tag_own[...] = jnp.broadcast_to(tag_of, (8, LANES))
    to_idx.wait()
    amp_copies[1].start()
    int_copy.start()
    for c in gap_copies:
        c.start()

    def pack_tiles(j, o):
        for s in range(CAP):
            slot = jnp.clip(idx_s[0, place_of(o) * CAP + s], 0, slots - 1)
            tile = amp_first[slot] if j == 0 else amp_rest[slot, pl.ds(STARTS[j] - first, SIZES[j]), :]
            if o == REACH:
                recv[j][REMOTE + s] = tile
            else:
                pack[j][place_of(o) * CAP + s] = tile

    def send_tiles(j, o):
        there = pl.ds(place_of(o) * CAP, CAP)
        pltpu.make_async_remote_copy(
            src_ref=pack[j].at[there], dst_ref=recv[j].at[there], send_sem=tile_send.at[j], recv_sem=tile_recv.at[j],
            device_id=(pair_of[o], v), device_id_type=MESH).start()

    amp_copies[0].wait()
    pack_tiles(0, PEERS[0])
    pl.semaphore_wait(barrier, len(PEERS) + n_virt - 1)
    send_tiles(0, PEERS[0])
    for o in PEERS[1:]:
        pack_tiles(0, o)
        send_tiles(0, o)
    for o in PEERS:
        pltpu.make_async_remote_copy(
            src_ref=tag_own, dst_ref=tags_in.at[place_of(o)], send_sem=tag_send, recv_sem=tag_recv,
            device_id=(pair_of[o], v), device_id_type=MESH).start()
    pack_tiles(0, REACH)
    amp_copies[1].wait()
    for j in range(1, CHUNKS):
        for o in PEERS:
            pack_tiles(j, o)
            if j < AHEAD:
                send_tiles(j, o)
        pack_tiles(j, REACH)

    wait_bytes(tags_in, tag_recv)
    wait_bytes(tags_in, tag_send)
    lane8 = lane[:8]
    tag8 = jnp.full((8, LANES), none, jnp.float32)
    for o in range(WINDOW):
        got = tag_own[...] if o == WINDOW - 1 else tags_in[o]
        tag8 = jnp.where((lane8 >= o * CAP) & (lane8 < (o + 1) * CAP), got, tag8)
    tag_r = jnp.broadcast_to(tag8[0:1, :], (LANES, LANES))
    tag_c = tag_r.T
    key_r = tag_r * LANES + lane
    key_c = tag_c * LANES + sub
    rank_c = jnp.sum(jnp.where(key_r < key_c, 1.0, 0.0), axis=1, keepdims=True)
    again_c = jnp.max(jnp.where((tag_r == tag_c) & (lane < sub), 1.0, 0.0), axis=1, keepdims=True)
    here = jnp.where(rank_c == lane, 1.0, 0.0)
    perm = jnp.sum(here * sub, axis=0, keepdims=True)
    again = jnp.sum(here * again_c, axis=0, keepdims=True)
    upto = jnp.sum(jnp.where(tag_c <= lane, 1.0, 0.0), axis=0, keepdims=True)
    equal = jnp.sum(jnp.where(tag_c == lane, 1.0, 0.0), axis=0, keepdims=True)
    last = jnp.where(equal > 0, upto - 1.0, float(CANDS))
    order[1] = jnp.zeros((8, LANES), jnp.int32)
    order[1, 0:1, :] = perm.astype(jnp.int32)
    order[1, 1:2, :] = again.astype(jnp.int32)
    order[1, 2:3, :] = last.astype(jnp.int32)
    to_order = pltpu.make_async_copy(order.at[1], order_s, order_sem)
    to_order.start()
    for c in gap_copies:
        c.wait()
    for r in range(row_count):
        gaps = rgap[pl.ds(r * edge, edge)].reshape(1, edge)
        rowmat[pl.ds(r * edge, edge), :] = jnp.broadcast_to(gaps, (edge, LANES)).T
    for j in range(CHUNKS):
        pref[j][CANDS] = jnp.zeros(pref[j].shape[1:], jnp.bfloat16)
    to_order.wait()

    def finish(j):
        wait_bytes(xrecv[j], x_recv.at[j])
        total = own[j][...]
        for t in range(1, n_virt):
            total = total + xrecv[j][t - 1].astype(jnp.float32)
        rows, col_gap = SIZES[j], cgap[...].reshape(1, cols)
        for r in range(row_count):
            row_gap = rowmat[pl.ds(r * edge + STARTS[j], rows), :]
            gap = jnp.concatenate([row_gap] * (cols // LANES), axis=1) + col_gap
            out_ref[pl.ds(r * edge + STARTS[j], rows), :] = total[r * rows:(r + 1) * rows] / gap

    send_order = (1, 3, 2, 0)
    for j in range(CHUNKS):
        if j + AHEAD < CHUNKS:
            wait_bytes(pack[j], tile_send.at[j])
            for o in PEERS:
                send_tiles(j + AHEAD, o)
        wait_bytes(recv[j].at[pl.ds(0, REMOTE)], tile_recv.at[j])
        rows = SIZES[j]

        acc = jnp.zeros((rows, LANES), jnp.float32)
        for at in range(CANDS):
            tile = recv[j][jnp.clip(order_s[0, at], 0, CANDS - 1)].astype(jnp.float32)
            acc = jnp.where(order_s[1, at] > 0, acc, 0.0) + tile
            pref[j][at] = acc.astype(jnp.bfloat16)
        for r in range(row_count):
            for k in range(k_count):
                block = pref[j][jnp.clip(order_s[2, r * k_count + k], 0, CANDS)]
                assembled[j][pl.ds(r * rows, rows), pl.ds(k * LANES, LANES)] = block
        for t in send_order:
            if j == 0 and t == send_order[0]:
                int_copy.wait()
            columns = pl.ds(pl.multiple_of(virt_of[t] * cols, cols), cols)
            part = jnp.dot(assembled[j][...], ints[:, columns], preferred_element_type=jnp.float32)
            if t == 0:
                own[j][...] = part
            else:
                xsend[j][t - 1] = part.astype(jnp.bfloat16)
                pltpu.make_async_remote_copy(
                    src_ref=xsend[j].at[t - 1], dst_ref=xrecv[j].at[t - 1], send_sem=x_send.at[j], recv_sem=x_recv.at[j],
                    device_id=(p, virt_of[t]), device_id_type=MESH).start()
        if j >= LAG:
            finish(j - LAG)
    for j in range(max(0, CHUNKS - LAG), CHUNKS):
        finish(j)
    for j in range(max(0, CHUNKS - AHEAD), CHUNKS):
        wait_bytes(pack[j], tile_send.at[j])
    for j in range(CHUNKS):
        wait_bytes(xsend[j], x_send.at[j])


def on_device(n_pair, n_virt, amplitudes, offsets, row_blocks, k_blocks, screen, integrals, row_gaps, col_gaps):
    slots, edge = amplitudes.shape[2], amplitudes.shape[3]
    k_count = integrals.shape[1] // edge
    row_count = row_gaps.shape[0] // edge
    cols = col_gaps.shape[0]

    def chunked(shape_of, dtype):
        return [pltpu.VMEM(shape_of(rows), dtype) for rows in SIZES]

    operands = (offsets[..., 0], row_blocks, k_blocks, screen, amplitudes, integrals, row_gaps, col_gaps)
    return pl.pallas_call(
        functools.partial(kernel, n_pair, n_virt, row_count, k_count),
        out_shape=jax.ShapeDtypeStruct((row_count * edge, cols), jnp.float32),
        in_specs=[pl.BlockSpec(memory_space=pltpu.HBM)] * 8,
        out_specs=pl.BlockSpec(memory_space=pltpu.VMEM),
        scratch_shapes=[
            pltpu.VMEM((slots, SIZES[0], edge), jnp.bfloat16),
            pltpu.VMEM((slots, edge - SIZES[0], edge), jnp.bfloat16),
            chunked(lambda rows: (REMOTE, rows, edge), jnp.bfloat16),
            chunked(lambda rows: (CANDS, rows, edge), jnp.bfloat16),
            chunked(lambda rows: (CANDS + 1, rows, edge), jnp.bfloat16),
            chunked(lambda rows: (row_count * rows, k_count * edge), jnp.bfloat16),
            chunked(lambda rows: (row_count * rows, cols), jnp.float32),
            chunked(lambda rows: (n_virt - 1, row_count * rows, cols), jnp.bfloat16),
            chunked(lambda rows: (n_virt - 1, row_count * rows, cols), jnp.bfloat16),
            pltpu.VMEM((k_count * edge, n_virt * cols), jnp.bfloat16),
            pltpu.VMEM((WINDOW - 1, 8, LANES), jnp.float32),
            pltpu.VMEM((8, LANES), jnp.float32),
            pltpu.VMEM((8, LANES), jnp.float32),
            pltpu.VMEM((4, 1, slots), jnp.int32),
            pltpu.VMEM((row_count * edge,), jnp.float32),
            pltpu.VMEM((cols,), jnp.float32),
            pltpu.VMEM((row_count * edge, LANES), jnp.float32),
            pltpu.VMEM((2, 8, LANES), jnp.int32),
            pltpu.SMEM((8, LANES), jnp.int32),
            pltpu.SMEM((8, LANES), jnp.int32),
            pltpu.SemaphoreType.DMA((2,)),
            pltpu.SemaphoreType.DMA,
            pltpu.SemaphoreType.DMA((4,)),
            pltpu.SemaphoreType.DMA((2,)),
            pltpu.SemaphoreType.DMA,
            pltpu.SemaphoreType.DMA,
            pltpu.SemaphoreType.DMA,
            pltpu.SemaphoreType.DMA((CHUNKS,)),
            pltpu.SemaphoreType.DMA((CHUNKS,)),
            pltpu.SemaphoreType.DMA((CHUNKS,)),
            pltpu.SemaphoreType.DMA((CHUNKS,)),
        ],
        compiler_params=pltpu.CompilerParams(
            collective_id=0, has_side_effects=True, vmem_limit_bytes=40 * 1024 * 1024),
        name="cycle",
    )(*[pltpu.with_memory_space_constraint(x, pltpu.HBM) for x in operands])


def solution(mesh):
    return jax.shard_map(
        functools.partial(on_device, mesh.shape["pair"], mesh.shape["virt"]),
        mesh=mesh,
        in_specs=(
            P("pair", "virt", None, None, None),
            P("pair", "virt", None, None),
            P("pair", "virt", None),
            P("pair", "virt", None),
            P("pair", "virt", None),
            P("pair", "virt", None),
            P("pair"),
            P("virt"),
        ),
        out_specs=P("pair", "virt"),
        check_vma=False,
    )
```
